32 devices in a mesh: node: 8 (over y, x, core), local: 4 (over z).
Axes of the slice: x: 2, y: 2, z: 4, core: 2. Of those that a mesh axis runs over, the one named last changes fastest.
Arguments:
- tokens: bfloat16 [8192, 3072], P(('node', 'local')), may hold values from -6 to 6
- out_grad: bfloat16 [8192, 512], P(('node', 'local')), may hold values from -6 to 6
- weights: bfloat16 [3072, 512], P(('node', 'local')), may hold values from -0.109375 to 0.109375
Outputs:
- projected: bfloat16 [8192, 512], P(('node', 'local'))
- input_grad: bfloat16 [8192, 3072], P(('node', 'local'))
- weight_grad: bfloat16 [3072, 512], P(('node', 'local'))
The draws below stay inside these ranges and needn't reach their ends.
All inputs are finite; a program needn't handle non-finite values.
Results may differ from the reference program's by a relative error of at most 0.005.
Values may be sent and summed in bfloat16 or wider, within the bound.
A program may use at most 64 MiB of HBM per device.

```python
import jax
import jax.numpy as jnp
from jax import lax

D = 3072
KVW = 512
TOK_DEV = 256
TOKENS = 8192


def spiked(result, stream_key, source, target, parts, factor):
    owner, partner = [(jnp.arange(result.shape[position]) // (result.shape[position] // parts)).reshape([-1 if axis == position else 1 for axis in range(result.ndim)]) for position in (source, target)]
    chosen = jax.random.permutation(stream_key, parts)[partner]
    strong = (owner == chosen) | (owner == (partner + parts // 2) % parts)
    return jnp.where(strong, factor * result, result)


def block_scale(stream_key, dims, pieces, smallest, largest):
    gain, own = 1.0, jax.random.fold_in(stream_key, 6)
    for dim, blocks in pieces:
        draws = jnp.exp(jax.random.uniform(jax.random.fold_in(own, dim), (blocks,), jnp.float32, smallest / len(pieces), largest / len(pieces)))
        gain = gain * jnp.repeat(draws, dims[dim] // blocks).reshape([-1 if axis == dim else 1 for axis in range(len(dims))])
    return gain


def centred(rng, dims, deviation, bound, split=(), kind=jnp.bfloat16):
    entries = deviation * jax.random.normal(rng, dims, jnp.float32)
    if split:
        entries = entries * block_scale(rng, dims, split, -0.22, 0.18)
    return jnp.clip(entries, -bound, bound).astype(kind)


def gaussian_with(stream_key, extent, width, limit, split, heavy, kind=jnp.bfloat16):
    entries = width * jax.random.normal(stream_key, extent, jnp.float32)
    if split:
        entries = entries * block_scale(stream_key, extent, split, -0.22, 0.18)
    return jnp.clip(spiked(entries, jax.random.fold_in(stream_key, 3), *heavy), -limit, limit).astype(kind)


def setup_inputs(seed: int = 0) -> dict:
    seeds = jax.random.split(jax.random.key(seed), 4)
    return {
        "tokens": gaussian_with(seeds[0], (TOKENS, D), 1.0, 6.0, ((0, 32),), (0, 1, 32, 2.75)),
        "out_grad": centred(seeds[1], (TOKENS, KVW), 1.0, 6.0, ((0, 32),)),
        "weights": centred(seeds[2], (D, KVW), D ** -0.5, 0.109375, ((0, 32),)),
    }


def reference(tokens, out_grad, weights):
    grad_scale = 1.0 / jnp.sqrt(jnp.float32(TOKENS))
    block_count = TOKENS // TOK_DEV
    tok_blocks = tokens.reshape(block_count, TOK_DEV, D)
    grad_blocks = out_grad.reshape(block_count, TOK_DEV, KVW)
    contract_cols = (((1,), (1,)), ((), ()))
    contract_rows = (((0,), (0,)), ((), ()))

    def block_step(totals, inputs):
        tok_block, grad_block = inputs
        keys_block = jnp.dot(tok_block, weights, preferred_element_type=jnp.float32).astype(jnp.bfloat16)
        backward = lax.dot_general(grad_block, weights, contract_cols, preferred_element_type=jnp.float32).astype(jnp.bfloat16)
        grad_term = lax.dot_general(tok_block, grad_block, contract_rows, preferred_element_type=jnp.float32)
        grad_term = (grad_term * grad_scale).astype(jnp.bfloat16)
        grad_term = lax.optimization_barrier(grad_term)
        return (totals + grad_term.astype(jnp.float32), (keys_block, backward))
    start_totals = jnp.zeros((D, KVW), jnp.float32)
    totals, outputs = lax.scan(block_step, start_totals, (tok_blocks, grad_blocks))
    keys_all, backward_all = outputs
    return (keys_all.reshape(TOKENS, KVW), backward_all.reshape(TOKENS, D), totals.astype(jnp.bfloat16))
```

```python
import functools

import jax
import jax.numpy as jnp
from jax import lax
from jax.experimental import pallas as pl
from jax.experimental.pallas import tpu as pltpu
from jax.sharding import PartitionSpec as P

ROWS_ROWS = (((0,), (0,)), ((), ()))
COLS_COLS = (((1,), (1,)), ((), ()))
MESH = pl.DeviceIdType.MESH


def kernel(scale, tok_h, og_h, w_h, proj_o, ig_h, wg_o,
           tok, og, tsib, osib, wf, acc, ig,
           g1b, g2a, g3, sA, sB, rA, rB, s2, r2, zs, zr,
           lsem, ssem, rsem, osem):
    f32, bf16 = jnp.float32, jnp.bfloat16
    node, z = lax.axis_index("node"), lax.axis_index("local")
    c = node % 2
    x = (node // 2) % 2
    y = node // 4
    rows, width = w_h.shape
    group = 4 * rows
    half = width // 2
    nx = node + 2 - 4 * x
    ny = node + 4 - 8 * y
    nd = nx + 4 - 8 * y
    sib = 1 - 2 * c
    dev_x, dev_y, dev_c = (nx, z), (ny, z), (node + sib, z)
    dev_z = [None] + [(node, (z + k) % 4) for k in (1, 2, 3)]
    quad = (node, nx, ny, nd)
    zq = [z] + [(z - k + 4) % 4 for k in (1, 2, 3)]

    def cols(n):
        return pl.ds(pl.multiple_of(n * group, 128), group)

    loads = [
        pltpu.make_async_copy(w_h, wf.at[node, z], lsem.at[0]),
        pltpu.make_async_copy(og_h, og, lsem.at[1]),
        pltpu.make_async_copy(tok_h, tok, lsem.at[2]),
    ]
    for load in loads:
        load.start()

    count = [0]
    started = []

    def remote(src, dst, device):
        i = count[0]
        count[0] += 1
        copy = pltpu.make_async_remote_copy(
            src_ref=src, dst_ref=dst, send_sem=ssem.at[i], recv_sem=rsem.at[i],
            device_id=device, device_id_type=MESH)
        started.append(copy)
        return copy

    barrier = pltpu.get_barrier_semaphore()
    for device in (dev_x, dev_y, dev_c, dev_z[1], dev_z[2], dev_z[3]):
        pl.semaphore_signal(barrier, inc=1, device_id=device, device_id_type=MESH)
    pl.semaphore_wait(barrier, 6)

    og_x = remote(og_h, osib, dev_c)
    og_x.start()
    order = (nd, nx, ny, node)
    tok_x = [remote(tok_h.at[:, cols(n + sib)], tsib.at[i], dev_c) for i, n in enumerate(order)]
    tok_x[0].start()
    wz = {k: remote(w_h, wf.at[node, z], dev_z[k]) for k in (1, 3, 2)}
    for k in (1, 3, 2):
        wz[k].start()
    for i in (1, 2, 3):
        tok_x[i].start()

    def spot(q, r):
        return wf.at[quad[q], zq[r]]

    wx, wy, wd, wc = {}, {}, {}, {}

    def to_sibling(q, r):
        wc[q, r] = remote(spot(q, r), spot(q, r), dev_c)
        wc[q, r].start()

    def send_own(r):
        wx[r] = remote(spot(0, r), spot(0, r), dev_x)
        wx[r].start()
        wy[r] = remote(spot(0, r), spot(0, r), dev_y)
        wy[r].start()
        to_sibling(0, r)

    loads[0].wait()
    send_own(0)

    def grad(i):
        part = lax.dot_general(tok[:, cols(order[i])], og[...], ROWS_ROWS, preferred_element_type=f32)
        part += lax.dot_general(tsib[i], osib[...], ROWS_ROWS, preferred_element_type=f32)
        return part * scale

    loads[1].wait()
    loads[2].wait()
    og_x.wait_recv()

    a1 = [remote(sA.at[i], rA.at[i], dev_x) for i in (0, 1)]
    b1 = [remote(sB.at[i], rB.at[i], dev_y) for i in (0, 1)]
    tok_x[0].wait_recv()
    g = grad(0)
    sA[0] = g[:, :half].astype(bf16)
    a1[0].start()
    sB[0] = g[:, half:].astype(bf16)
    b1[0].start()
    tok_x[1].wait_recv()
    g = grad(1)
    sA[1] = g[:, :half].astype(bf16)
    a1[1].start()
    g1b[...] = g[:, half:]
    tok_x[2].wait_recv()
    g = grad(2)
    sB[1] = g[:, half:].astype(bf16)
    b1[1].start()
    g2a[...] = g[:, :half]
    tok_x[3].wait_recv()
    g3[...] = grad(3)

    for k in (1, 3, 2):
        wz[k].wait_recv()
        send_own(k)

    def relay(r):
        wx[r].wait_recv()
        if r % 2 == 0:
            wd[r] = remote(spot(1, r), spot(1, r), dev_y)
            wd[r].start()
        to_sibling(1, r)
        wy[r].wait_recv()
        if r % 2 == 1:
            wd[r] = remote(spot(2, r), spot(2, r), dev_x)
            wd[r].start()
        to_sibling(2, r)

    relay(0)

    a2 = remote(s2.at[0], r2.at[0], dev_y)
    b2 = remote(s2.at[1], r2.at[1], dev_x)
    a1[0].wait_recv()
    s2[0] = (g2a[...] + rA[0].astype(f32)).astype(bf16)
    a2.start()
    b1[0].wait_recv()
    s2[1] = (g1b[...] + rB[0].astype(f32)).astype(bf16)
    b2.start()

    stores = []

    def use(n, first=False):
        w = wf[n].reshape(group, width)
        part = jnp.dot(tok[:, cols(n)], w, preferred_element_type=f32)
        if first:
            acc[...] = part
        else:
            acc[...] += part
        i = len(stores)
        ig[i] = lax.dot_general(og[...], w, COLS_COLS, preferred_element_type=f32).astype(bf16)
        store = pltpu.make_async_copy(ig.at[i], ig_h.at[:, cols(n)], osem.at[i])
        store.start()
        stores.append(store)

    def use_sibling(q):
        for r in range(4):
            wc[q, r].wait_recv()
        use(quad[q] + sib)

    use(node, True)
    a1[1].wait_recv()
    g3[:, :half] += rA[1].astype(f32)
    b1[1].wait_recv()
    g3[:, half:] += rB[1].astype(f32)

    relay(1)
    use_sibling(0)

    a2.wait_recv()
    g3[:, :half] += r2[0].astype(f32)
    b2.wait_recv()
    g3[:, half:] += r2[1].astype(f32)
    zs[...] = g3[...].astype(bf16).reshape(4, rows, width)
    gz = {}
    for k in (1, 3, 2):
        gz[k] = remote(zs.at[(z + k) % 4], zr.at[k - 1], dev_z[k])
        gz[k].start()

    relay(3)
    relay(2)
    for r in (0, 1, 3, 2):
        wd[r].wait_recv()
        to_sibling(3, r)
    use(nx)
    use(ny)
    use_sibling(1)
    use_sibling(2)

    for k in (1, 3, 2):
        gz[k].wait_recv()
    own = g3[pl.ds(pl.multiple_of(z * rows, 16), rows), :]
    wg_o[...] = (own + zr[0].astype(f32) + zr[1].astype(f32) + zr[2].astype(f32)).astype(bf16)

    use(nd)
    use_sibling(3)
    proj_o[...] = acc[...].astype(bf16)

    for copy in started:
        copy.wait_send()
    for store in stores:
        store.wait()


COPIES = 1 + 4 + 3 + 4 + 4 + 4 + 16 + 4 + 2 + 3


def fused(tokens, out_grad, weights):
    toks, features = tokens.shape
    rows, width = weights.shape
    devices = lax.axis_size("node") * lax.axis_size("local")
    scale = 1.0 / float(toks * devices) ** 0.5
    group, half = 4 * rows, width // 2
    bf16, f32 = jnp.bfloat16, jnp.float32
    return pl.pallas_call(
        functools.partial(kernel, scale),
        out_shape=(
            jax.ShapeDtypeStruct((toks, width), bf16),
            jax.ShapeDtypeStruct((toks, features), bf16),
            jax.ShapeDtypeStruct((rows, width), bf16),
        ),
        in_specs=[pl.BlockSpec(memory_space=pl.ANY)] * 3,
        out_specs=(
            pl.BlockSpec(memory_space=pltpu.VMEM),
            pl.BlockSpec(memory_space=pl.ANY),
            pl.BlockSpec(memory_space=pltpu.VMEM),
        ),
        scratch_shapes=[
            pltpu.VMEM((toks, features), bf16),
            pltpu.VMEM((toks, width), bf16),
            pltpu.VMEM((4, toks, group), bf16),
            pltpu.VMEM((toks, width), bf16),
            pltpu.VMEM((8, 4, rows, width), bf16),
            pltpu.VMEM((toks, width), f32),
            pltpu.VMEM((8, toks, group), bf16),
            pltpu.VMEM((group, half), f32),
            pltpu.VMEM((group, half), f32),
            pltpu.VMEM((group, width), f32),
            pltpu.VMEM((2, group, half), bf16),
            pltpu.VMEM((2, group, half), bf16),
            pltpu.VMEM((2, group, half), bf16),
            pltpu.VMEM((2, group, half), bf16),
            pltpu.VMEM((2, group, half), bf16),
            pltpu.VMEM((2, group, half), bf16),
            pltpu.VMEM((4, rows, width), bf16),
            pltpu.VMEM((3, rows, width), bf16),
            pltpu.SemaphoreType.DMA((3,)),
            pltpu.SemaphoreType.DMA((COPIES,)),
            pltpu.SemaphoreType.DMA((COPIES,)),
            pltpu.SemaphoreType.DMA((8,)),
        ],
        compiler_params=pltpu.CompilerParams(
            collective_id=0, has_side_effects=True, vmem_limit_bytes=40 * 2**20),
        cost_estimate=pl.CostEstimate(
            flops=6 * toks * features * width, bytes_accessed=2 * toks * features * 4, transcendentals=0),
    )(tokens, out_grad, weights)


def plain(tokens, out_grad, weights):
    tok_rows = tokens.shape[0]
    devices = lax.axis_size("node") * lax.axis_size("local")
    grad_scale = 1.0 / jnp.sqrt(jnp.float32(tok_rows * devices))
    grad_term = lax.dot_general(tokens, out_grad, ROWS_ROWS, preferred_element_type=jnp.float32)
    grad_term = (grad_term * grad_scale).astype(jnp.bfloat16)
    grad_term = lax.optimization_barrier(grad_term).astype(jnp.float32)
    shard_rows = lax.all_gather(weights, ("node", "local"), axis=0, tiled=True)
    projected = jnp.dot(tokens, shard_rows, preferred_element_type=jnp.float32).astype(jnp.bfloat16)
    input_grad = lax.dot_general(
        out_grad, shard_rows, COLS_COLS, preferred_element_type=jnp.float32).astype(jnp.bfloat16)
    across = lax.psum_scatter(grad_term, "node", scatter_dimension=0, tiled=True)
    summed = lax.psum_scatter(across, "local", scatter_dimension=0, tiled=True)
    return projected, input_grad, summed.astype(jnp.bfloat16)


def solution(mesh):
    spec = P(("node", "local"), None)
    fits = mesh.shape["node"] == 8 and mesh.shape["local"] == 4
    return jax.shard_map(
        fused if fits else plain,
        mesh=mesh,
        in_specs=(spec, spec, spec),
        out_specs=(spec, spec, spec),
        check_vma=False,
    )
```

```python
import functools

import jax
import jax.numpy as jnp
from jax import lax
from jax.experimental import pallas as pl
from jax.experimental.pallas import tpu as pltpu
from jax.sharding import PartitionSpec as P

ROWS_ROWS = (((0,), (0,)), ((), ()))
COLS_COLS = (((1,), (1,)), ((), ()))
MESH = pl.DeviceIdType.MESH


def kernel(scale, tok_h, og_h, w_h, proj_o, ig_h, wg_o,
           tok, og, tsib, osib, wf, acc, ig,
           g1b, g2a, g3, sA, sB, rA, rB, s2, r2, zs, zr,
           lsem, ssem, rsem, osem):
    f32, bf16 = jnp.float32, jnp.bfloat16
    node, z = lax.axis_index("node"), lax.axis_index("local")
    c = node % 2
    x = (node // 2) % 2
    y = node // 4
    rows, width = w_h.shape
    group = 4 * rows
    half = width // 2
    nx = node + 2 - 4 * x
    ny = node + 4 - 8 * y
    nd = nx + 4 - 8 * y
    sib = 1 - 2 * c
    dev_x, dev_y, dev_c = (nx, z), (ny, z), (node + sib, z)
    dev_z = [None] + [(node, (z + k) % 4) for k in (1, 2, 3)]
    quad = (node, nx, ny, nd)
    zq = [z] + [(z - k + 4) % 4 for k in (1, 2, 3)]

    def cols(n):
        return pl.ds(pl.multiple_of(n * group, 128), group)

    loads = [
        pltpu.make_async_copy(w_h, wf.at[node, z], lsem.at[0]),
        pltpu.make_async_copy(og_h, og, lsem.at[1]),
        pltpu.make_async_copy(tok_h, tok, lsem.at[2]),
    ]
    for load in loads:
        load.start()

    count = [0]
    started = []

    def remote(src, dst, device):
        i = count[0]
        count[0] += 1
        copy = pltpu.make_async_remote_copy(
            src_ref=src, dst_ref=dst, send_sem=ssem.at[i], recv_sem=rsem.at[i],
            device_id=device, device_id_type=MESH)
        started.append(copy)
        return copy

    barrier = pltpu.get_barrier_semaphore()
    for device in (dev_x, dev_y, dev_c, dev_z[1], dev_z[2], dev_z[3]):
        pl.semaphore_signal(barrier, inc=1, device_id=device, device_id_type=MESH)
    pl.semaphore_wait(barrier, 6)

    og_x = remote(og_h, osib, dev_c)
    og_x.start()
    order = (nd, nx, ny, node)
    tok_x = [remote(tok_h.at[:, cols(n + sib)], tsib.at[i], dev_c) for i, n in enumerate(order)]
    tok_x[0].start()
    wz = {k: remote(w_h, wf.at[node, z], dev_z[k]) for k in (1, 3, 2)}
    for k in (1, 3, 2):
        wz[k].start()
    for i in (1, 2, 3):
        tok_x[i].start()

    def spot(q, r):
        return wf.at[quad[q], zq[r]]

    wx, wy, wd, wc = {}, {}, {}, {}

    def to_sibling(q, r):
        wc[q, r] = remote(spot(q, r), spot(q, r), dev_c)
        wc[q, r].start()

    def send_own(r):
        wx[r] = remote(spot(0, r), spot(0, r), dev_x)
        wx[r].start()
        wy[r] = remote(spot(0, r), spot(0, r), dev_y)
        wy[r].start()
        to_sibling(0, r)

    loads[0].wait()
    send_own(0)

    def grad(i):
        part = lax.dot_general(tok[:, cols(order[i])], og[...], ROWS_ROWS, preferred_element_type=f32)
        part += lax.dot_general(tsib[i], osib[...], ROWS_ROWS, preferred_element_type=f32)
        return part * scale

    loads[1].wait()
    loads[2].wait()
    og_x.wait_recv()

    a1 = [remote(sA.at[i], rA.at[i], dev_x) for i in (0, 1)]
    b1 = [remote(sB.at[i], rB.at[i], dev_y) for i in (0, 1)]
    tok_x[0].wait_recv()
    g = grad(0)
    sA[0] = g[:, :half].astype(bf16)
    a1[0].start()
    sB[0] = g[:, half:].astype(bf16)
    b1[0].start()
    tok_x[1].wait_recv()
    g = grad(1)
    sA[1] = g[:, :half].astype(bf16)
    a1[1].start()
    g1b[...] = g[:, half:]
    tok_x[2].wait_recv()
    g = grad(2)
    sB[1] = g[:, half:].astype(bf16)
    b1[1].start()
    g2a[...] = g[:, :half]
    tok_x[3].wait_recv()
    g3[...] = grad(3)

    def relay(r):
        wx[r].wait_recv()
        if r % 2 == 0:
            wd[r] = remote(spot(1, r), spot(1, r), dev_y)
            wd[r].start()
        to_sibling(1, r)
        wy[r].wait_recv()
        if r % 2 == 1:
            wd[r] = remote(spot(2, r), spot(2, r), dev_x)
            wd[r].start()
        to_sibling(2, r)

    a2 = remote(s2.at[0], r2.at[0], dev_y)
    b2 = remote(s2.at[1], r2.at[1], dev_x)
    a1[0].wait_recv()
    s2[0] = (g2a[...] + rA[0].astype(f32)).astype(bf16)
    a2.start()
    b1[0].wait_recv()
    s2[1] = (g1b[...] + rB[0].astype(f32)).astype(bf16)
    b2.start()

    for k in (1, 3, 2):
        wz[k].wait_recv()
        send_own(k)

    relay(0)

    stores = []

    def use(n, first=False):
        w = wf[n].reshape(group, width)
        part = jnp.dot(tok[:, cols(n)], w, preferred_element_type=f32)
        if first:
            acc[...] = part
        else:
            acc[...] += part
        i = len(stores)
        ig[i] = lax.dot_general(og[...], w, COLS_COLS, preferred_element_type=f32).astype(bf16)
        store = pltpu.make_async_copy(ig.at[i], ig_h.at[:, cols(n)], osem.at[i])
        store.start()
        stores.append(store)

    def use_sibling(q):
        for r in range(4):
            wc[q, r].wait_recv()
        use(quad[q] + sib)

    a1[1].wait_recv()
    g3[:, :half] += rA[1].astype(f32)
    b1[1].wait_recv()
    g3[:, half:] += rB[1].astype(f32)

    a2.wait_recv()
    g3[:, :half] += r2[0].astype(f32)
    b2.wait_recv()
    g3[:, half:] += r2[1].astype(f32)
    zs[...] = g3[...].astype(bf16).reshape(4, rows, width)
    gz = {}
    for k in (1, 3, 2):
        gz[k] = remote(zs.at[(z + k) % 4], zr.at[k - 1], dev_z[k])
        gz[k].start()

    relay(1)
    relay(3)
    relay(2)
    use(node, True)
    use_sibling(0)
    for r in (0, 1, 3, 2):
        wd[r].wait_recv()
        to_sibling(3, r)
    use(nx)
    use(ny)
    use_sibling(1)
    use_sibling(2)

    for k in (1, 3, 2):
        gz[k].wait_recv()
    own = g3[pl.ds(pl.multiple_of(z * rows, 16), rows), :]
    wg_o[...] = (own + zr[0].astype(f32) + zr[1].astype(f32) + zr[2].astype(f32)).astype(bf16)

    use(nd)
    use_sibling(3)
    proj_o[...] = acc[...].astype(bf16)

    for copy in started:
        copy.wait_send()
    for store in stores:
        store.wait()


COPIES = 1 + 4 + 3 + 4 + 4 + 4 + 16 + 4 + 2 + 3


def fused(tokens, out_grad, weights):
    toks, features = tokens.shape
    rows, width = weights.shape
    devices = lax.axis_size("node") * lax.axis_size("local")
    scale = 1.0 / float(toks * devices) ** 0.5
    group, half = 4 * rows, width // 2
    bf16, f32 = jnp.bfloat16, jnp.float32
    return pl.pallas_call(
        functools.partial(kernel, scale),
        out_shape=(
            jax.ShapeDtypeStruct((toks, width), bf16),
            jax.ShapeDtypeStruct((toks, features), bf16),
            jax.ShapeDtypeStruct((rows, width), bf16),
        ),
        in_specs=[pl.BlockSpec(memory_space=pltpu.HBM)] * 3,
        out_specs=(
            pl.BlockSpec(memory_space=pltpu.VMEM),
            pl.BlockSpec(memory_space=pl.ANY),
            pl.BlockSpec(memory_space=pltpu.VMEM),
        ),
        scratch_shapes=[
            pltpu.VMEM((toks, features), bf16),
            pltpu.VMEM((toks, width), bf16),
            pltpu.VMEM((4, toks, group), bf16),
            pltpu.VMEM((toks, width), bf16),
            pltpu.VMEM((8, 4, rows, width), bf16),
            pltpu.VMEM((toks, width), f32),
            pltpu.VMEM((8, toks, group), bf16),
            pltpu.VMEM((group, half), f32),
            pltpu.VMEM((group, half), f32),
            pltpu.VMEM((group, width), f32),
            pltpu.VMEM((2, group, half), bf16),
            pltpu.VMEM((2, group, half), bf16),
            pltpu.VMEM((2, group, half), bf16),
            pltpu.VMEM((2, group, half), bf16),
            pltpu.VMEM((2, group, half), bf16),
            pltpu.VMEM((2, group, half), bf16),
            pltpu.VMEM((4, rows, width), bf16),
            pltpu.VMEM((3, rows, width), bf16),
            pltpu.SemaphoreType.DMA((3,)),
            pltpu.SemaphoreType.DMA((COPIES,)),
            pltpu.SemaphoreType.DMA((COPIES,)),
            pltpu.SemaphoreType.DMA((8,)),
        ],
        compiler_params=pltpu.CompilerParams(
            collective_id=0, has_side_effects=True, vmem_limit_bytes=40 * 2**20),
        cost_estimate=pl.CostEstimate(
            flops=6 * toks * features * width, bytes_accessed=2 * toks * features * 4, transcendentals=0),
    )(tokens, out_grad, weights)


def plain(tokens, out_grad, weights):
    tok_rows = tokens.shape[0]
    devices = lax.axis_size("node") * lax.axis_size("local")
    grad_scale = 1.0 / jnp.sqrt(jnp.float32(tok_rows * devices))
    grad_term = lax.dot_general(tokens, out_grad, ROWS_ROWS, preferred_element_type=jnp.float32)
    grad_term = (grad_term * grad_scale).astype(jnp.bfloat16)
    grad_term = lax.optimization_barrier(grad_term).astype(jnp.float32)
    shard_rows = lax.all_gather(weights, ("node", "local"), axis=0, tiled=True)
    projected = jnp.dot(tokens, shard_rows, preferred_element_type=jnp.float32).astype(jnp.bfloat16)
    input_grad = lax.dot_general(
        out_grad, shard_rows, COLS_COLS, preferred_element_type=jnp.float32).astype(jnp.bfloat16)
    across = lax.psum_scatter(grad_term, "node", scatter_dimension=0, tiled=True)
    summed = lax.psum_scatter(across, "local", scatter_dimension=0, tiled=True)
    return projected, input_grad, summed.astype(jnp.bfloat16)


def solution(mesh):
    spec = P(("node", "local"), None)
    fits = mesh.shape["node"] == 8 and mesh.shape["local"] == 4
    return jax.shard_map(
        fused if fits else plain,
        mesh=mesh,
        in_specs=(spec, spec, spec),
        out_specs=(spec, spec, spec),
        check_vma=False,
    )
```

```python
import functools

import jax
import jax.numpy as jnp
from jax import lax
from jax.experimental import pallas as pl
from jax.experimental.pallas import tpu as pltpu
from jax.sharding import PartitionSpec as P

ROWS_ROWS = (((0,), (0,)), ((), ()))
COLS_COLS = (((1,), (1,)), ((), ()))
MESH = pl.DeviceIdType.MESH


def kernel(scale, tok_h, og_h, w_h, proj_o, ig_h, wg_o,
           tok, og, tsib, osib, wf, acc, ig,
           g1b, g2a, g3, sA, sB, rA, rB, s2, r2, zs, zr,
           lsem, ssem, rsem, osem):
    f32, bf16 = jnp.float32, jnp.bfloat16
    node, z = lax.axis_index("node"), lax.axis_index("local")
    c = node % 2
    x = (node // 2) % 2
    y = node // 4
    rows, width = w_h.shape
    group = 4 * rows
    half = width // 2
    nx = node + 2 - 4 * x
    ny = node + 4 - 8 * y
    nd = nx + 4 - 8 * y
    sib = 1 - 2 * c
    dev_x, dev_y, dev_c = (nx, z), (ny, z), (node + sib, z)
    dev_z = [None] + [(node, (z + k) % 4) for k in (1, 2, 3)]
    quad = (node, nx, ny, nd)
    zq = [z] + [(z - k + 4) % 4 for k in (1, 2, 3)]

    def cols(n):
        return pl.ds(pl.multiple_of(n * group, 128), group)

    loads = [
        pltpu.make_async_copy(w_h, wf.at[node, z], lsem.at[0]),
        pltpu.make_async_copy(og_h, og, lsem.at[1]),
        pltpu.make_async_copy(tok_h, tok, lsem.at[2]),
    ]
    for load in loads:
        load.start()

    count = [0]
    started = []

    def remote(src, dst, device):
        i = count[0]
        count[0] += 1
        copy = pltpu.make_async_remote_copy(
            src_ref=src, dst_ref=dst, send_sem=ssem.at[i], recv_sem=rsem.at[i],
            device_id=device, device_id_type=MESH)
        started.append(copy)
        return copy

    barrier = pltpu.get_barrier_semaphore()
    for device in (dev_x, dev_y, dev_c, dev_z[1], dev_z[2], dev_z[3]):
        pl.semaphore_signal(barrier, inc=1, device_id=device, device_id_type=MESH)
    pl.semaphore_wait(barrier, 6)

    og_x = remote(og_h, osib, dev_c)
    og_x.start()
    order = (nd, nx, ny, node)
    tok_x = [remote(tok_h.at[:, cols(n + sib)], tsib.at[i], dev_c) for i, n in enumerate(order)]
    tok_x[0].start()
    wz = {k: remote(w_h, wf.at[node, z], dev_z[k]) for k in (1, 3, 2)}
    for k in (1, 3, 2):
        wz[k].start()
    for i in (1, 2, 3):
        tok_x[i].start()

    def spot(q, r):
        return wf.at[quad[q], zq[r]]

    wx, wy, wd, wc = {}, {}, {}, {}

    def to_sibling(q, r):
        wc[q, r] = remote(spot(q, r), spot(q, r), dev_c)
        wc[q, r].start()

    def send_own(r):
        wx[r] = remote(spot(0, r), spot(0, r), dev_x)
        wx[r].start()
        wy[r] = remote(spot(0, r), spot(0, r), dev_y)
        wy[r].start()
        to_sibling(0, r)

    loads[0].wait()
    send_own(0)

    def grad(i):
        part = lax.dot_general(tok[:, cols(order[i])], og[...], ROWS_ROWS, preferred_element_type=f32)
        part += lax.dot_general(tsib[i], osib[...], ROWS_ROWS, preferred_element_type=f32)
        return part * scale

    def relay(r):
        wx[r].wait_recv()
        to_sibling(1, r)
        wy[r].wait_recv()
        to_sibling(2, r)

    def diagonal():
        low, high = pl.ds(0, rows // 2), pl.ds(rows // 2, rows // 2)
        wx[0].wait_recv()
        part = wf.at[nx, z, low]
        d_low = remote(part, part, dev_y)
        d_low.start()
        wy[0].wait_recv()
        part = wf.at[ny, z, high]
        d_high = remote(part, part, dev_x)
        d_high.start()
        return d_low, d_high

    def diagonal_along_z():
        d_low.wait_recv()
        d_high.wait_recv()
        for k in (1, 3, 2):
            wd[k] = remote(spot(3, 0), spot(3, 0), dev_z[k])
            wd[k].start()
        to_sibling(1, 0)
        to_sibling(2, 0)
        to_sibling(3, 0)

    loads[1].wait()
    loads[2].wait()
    og_x.wait_recv()

    a1 = [remote(sA.at[i], rA.at[i], dev_x) for i in (0, 1)]
    b1 = [remote(sB.at[i], rB.at[i], dev_y) for i in (0, 1)]
    tok_x[0].wait_recv()
    g = grad(0)
    sA[0] = g[:, :half].astype(bf16)
    a1[0].start()
    sB[0] = g[:, half:].astype(bf16)
    b1[0].start()
    d_low, d_high = diagonal()
    tok_x[1].wait_recv()
    g = grad(1)
    sA[1] = g[:, :half].astype(bf16)
    a1[1].start()
    g1b[...] = g[:, half:]
    tok_x[2].wait_recv()
    g = grad(2)
    sB[1] = g[:, half:].astype(bf16)
    b1[1].start()
    g2a[...] = g[:, :half]
    tok_x[3].wait_recv()
    g3[...] = grad(3)

    a2 = remote(s2.at[0], r2.at[0], dev_y)
    b2 = remote(s2.at[1], r2.at[1], dev_x)
    a1[0].wait_recv()
    s2[0] = (g2a[...] + rA[0].astype(f32)).astype(bf16)
    a2.start()
    b1[0].wait_recv()
    s2[1] = (g1b[...] + rB[0].astype(f32)).astype(bf16)
    b2.start()

    for k in (1, 3, 2):
        wz[k].wait_recv()
        send_own(k)
    diagonal_along_z()


    stores = []

    def use(n, first=False):
        w = wf[n].reshape(group, width)
        part = jnp.dot(tok[:, cols(n)], w, preferred_element_type=f32)
        if first:
            acc[...] = part
        else:
            acc[...] += part
        i = len(stores)
        ig[i] = lax.dot_general(og[...], w, COLS_COLS, preferred_element_type=f32).astype(bf16)
        store = pltpu.make_async_copy(ig.at[i], ig_h.at[:, cols(n)], osem.at[i])
        store.start()
        stores.append(store)

    def use_sibling(q):
        for r in range(4):
            wc[q, r].wait_recv()
        use(quad[q] + sib)

    a1[1].wait_recv()
    g3[:, :half] += rA[1].astype(f32)
    b1[1].wait_recv()
    g3[:, half:] += rB[1].astype(f32)

    a2.wait_recv()
    g3[:, :half] += r2[0].astype(f32)
    b2.wait_recv()
    g3[:, half:] += r2[1].astype(f32)
    zs[...] = g3[...].astype(bf16).reshape(4, rows, width)
    gz = {}
    for k in (1, 3, 2):
        gz[k] = remote(zs.at[(z + k) % 4], zr.at[k - 1], dev_z[k])
        gz[k].start()

    relay(1)
    relay(3)
    relay(2)
    use(node, True)
    use_sibling(0)
    for r in (1, 3, 2):
        wd[r].wait_recv()
        to_sibling(3, r)
    use(nx)
    use(ny)
    use_sibling(1)
    use_sibling(2)

    for k in (1, 3, 2):
        gz[k].wait_recv()
    own = g3[pl.ds(pl.multiple_of(z * rows, 16), rows), :]
    wg_o[...] = (own + zr[0].astype(f32) + zr[1].astype(f32) + zr[2].astype(f32)).astype(bf16)

    use(nd)
    use_sibling(3)
    proj_o[...] = acc[...].astype(bf16)

    for copy in started:
        copy.wait_send()
    for store in stores:
        store.wait()


def hand_on(a, b, c, a_out, b_out, c_out, sem):
    pairs = ((a, a_out), (b, b_out), (c, c_out))
    copies = [pltpu.make_async_copy(src, dst, sem.at[i]) for i, (src, dst) in enumerate(pairs)]
    for copy in copies:
        copy.start()
    for copy in copies:
        copy.wait()


COPIES = 1 + 4 + 3 + 4 + 4 + 5 + 16 + 4 + 2 + 3


def fused(tokens, out_grad, weights):
    toks, features = tokens.shape
    rows, width = weights.shape
    devices = lax.axis_size("node") * lax.axis_size("local")
    scale = 1.0 / float(toks * devices) ** 0.5
    group, half = 4 * rows, width // 2
    bf16, f32 = jnp.bfloat16, jnp.float32
    results = pl.pallas_call(
        functools.partial(kernel, scale),
        out_shape=(
            jax.ShapeDtypeStruct((toks, width), bf16),
            jax.ShapeDtypeStruct((toks, features), bf16),
            jax.ShapeDtypeStruct((rows, width), bf16),
        ),
        in_specs=[pl.BlockSpec(memory_space=pltpu.HBM)] * 3,
        out_specs=(
            pl.BlockSpec(memory_space=pltpu.VMEM),
            pl.BlockSpec(memory_space=pl.ANY),
            pl.BlockSpec(memory_space=pltpu.VMEM),
        ),
        scratch_shapes=[
            pltpu.VMEM((toks, features), bf16),
            pltpu.VMEM((toks, width), bf16),
            pltpu.VMEM((4, toks, group), bf16),
            pltpu.VMEM((toks, width), bf16),
            pltpu.VMEM((8, 4, rows, width), bf16),
            pltpu.VMEM((toks, width), f32),
            pltpu.VMEM((8, toks, group), bf16),
            pltpu.VMEM((group, half), f32),
            pltpu.VMEM((group, half), f32),
            pltpu.VMEM((group, width), f32),
            pltpu.VMEM((2, group, half), bf16),
            pltpu.VMEM((2, group, half), bf16),
            pltpu.VMEM((2, group, half), bf16),
            pltpu.VMEM((2, group, half), bf16),
            pltpu.VMEM((2, group, half), bf16),
            pltpu.VMEM((2, group, half), bf16),
            pltpu.VMEM((4, rows, width), bf16),
            pltpu.VMEM((3, rows, width), bf16),
            pltpu.SemaphoreType.DMA((3,)),
            pltpu.SemaphoreType.DMA((COPIES,)),
            pltpu.SemaphoreType.DMA((COPIES,)),
            pltpu.SemaphoreType.DMA((8,)),
        ],
        compiler_params=pltpu.CompilerParams(
            collective_id=0, has_side_effects=True, vmem_limit_bytes=40 * 2**20),
        cost_estimate=pl.CostEstimate(
            flops=6 * toks * features * width, bytes_accessed=2 * toks * features * 4, transcendentals=0),
    )(tokens, out_grad, weights)
    return pl.pallas_call(
        hand_on,
        out_shape=tuple(jax.ShapeDtypeStruct(a.shape, a.dtype) for a in results),
        in_specs=[pl.BlockSpec(memory_space=pl.ANY)] * 3,
        out_specs=[pl.BlockSpec(memory_space=pl.ANY)] * 3,
        scratch_shapes=[pltpu.SemaphoreType.DMA((3,))],
        compiler_params=pltpu.CompilerParams(vmem_limit_bytes=2**20),
    )(*results)


def plain(tokens, out_grad, weights):
    tok_rows = tokens.shape[0]
    devices = lax.axis_size("node") * lax.axis_size("local")
    grad_scale = 1.0 / jnp.sqrt(jnp.float32(tok_rows * devices))
    grad_term = lax.dot_general(tokens, out_grad, ROWS_ROWS, preferred_element_type=jnp.float32)
    grad_term = (grad_term * grad_scale).astype(jnp.bfloat16)
    grad_term = lax.optimization_barrier(grad_term).astype(jnp.float32)
    shard_rows = lax.all_gather(weights, ("node", "local"), axis=0, tiled=True)
    projected = jnp.dot(tokens, shard_rows, preferred_element_type=jnp.float32).astype(jnp.bfloat16)
    input_grad = lax.dot_general(
        out_grad, shard_rows, COLS_COLS, preferred_element_type=jnp.float32).astype(jnp.bfloat16)
    across = lax.psum_scatter(grad_term, "node", scatter_dimension=0, tiled=True)
    summed = lax.psum_scatter(across, "local", scatter_dimension=0, tiled=True)
    return projected, input_grad, summed.astype(jnp.bfloat16)


def solution(mesh):
    spec = P(("node", "local"), None)
    fits = mesh.shape["node"] == 8 and mesh.shape["local"] == 4
    return jax.shard_map(
        fused if fits else plain,
        mesh=mesh,
        in_specs=(spec, spec, spec),
        out_specs=(spec, spec, spec),
        check_vma=False,
    )
```

```python
import functools

import jax
import jax.numpy as jnp
from jax import lax
from jax.experimental import pallas as pl
from jax.experimental.pallas import tpu as pltpu
from jax.sharding import PartitionSpec as P

ROWS_ROWS = (((0,), (0,)), ((), ()))
COLS_COLS = (((1,), (1,)), ((), ()))
MESH = pl.DeviceIdType.MESH


def kernel(scale, tok_h, og_h, w_h, proj_o, ig_h, wg_o,
           tok, og, tsib, osib, wf, acc, ig,
           g1b, g2a, g3, sA, sB, rA, rB, s2, r2, zs, zr,
           lsem, ssem, rsem, osem):
    f32, bf16 = jnp.float32, jnp.bfloat16
    node, z = lax.axis_index("node"), lax.axis_index("local")
    c = node % 2
    x = (node // 2) % 2
    y = node // 4
    rows, width = w_h.shape
    group = 4 * rows
    half = width // 2
    quarter = width // 4
    nx = node + 2 - 4 * x
    ny = node + 4 - 8 * y
    nd = nx + 4 - 8 * y
    sib = 1 - 2 * c
    dev_x, dev_y, dev_c = (nx, z), (ny, z), (node + sib, z)
    dev_z = [None] + [(node, (z + k) % 4) for k in (1, 2, 3)]
    quad = (node, nx, ny, nd)
    zq = [z] + [(z - k + 4) % 4 for k in (1, 2, 3)]

    def cols(n):
        return pl.ds(pl.multiple_of(n * group, 128), group)

    loads = [
        pltpu.make_async_copy(w_h, wf.at[node, z], lsem.at[0]),
        pltpu.make_async_copy(og_h, og, lsem.at[1]),
        pltpu.make_async_copy(tok_h, tok, lsem.at[2]),
    ]
    for load in loads:
        load.start()

    count = [0]
    started = []

    def remote(src, dst, device):
        i = count[0]
        count[0] += 1
        copy = pltpu.make_async_remote_copy(
            src_ref=src, dst_ref=dst, send_sem=ssem.at[i], recv_sem=rsem.at[i],
            device_id=device, device_id_type=MESH)
        started.append(copy)
        return copy

    barrier = pltpu.get_barrier_semaphore()
    for device in (dev_x, dev_y, dev_c, dev_z[1], dev_z[2], dev_z[3]):
        pl.semaphore_signal(barrier, inc=1, device_id=device, device_id_type=MESH)
    pl.semaphore_wait(barrier, 6)

    og_x = remote(og_h, osib, dev_c)
    og_x.start()
    order = (nd, nx, ny, node)
    tok_x = [remote(tok_h.at[:, cols(n + sib)], tsib.at[i], dev_c) for i, n in enumerate(order)]
    tok_x[0].start()
    wz = {k: remote(w_h, wf.at[node, z], dev_z[k]) for k in (1, 3, 2)}
    for k in (1, 3, 2):
        wz[k].start()
    for i in (1, 2, 3):
        tok_x[i].start()

    def spot(q, r):
        return wf.at[quad[q], zq[r]]

    wx, wy, wd, wc = {}, {}, {}, {}

    def to_sibling(q, r):
        wc[q, r] = remote(spot(q, r), spot(q, r), dev_c)
        wc[q, r].start()

    def send_own(r):
        wx[r] = remote(spot(0, r), spot(0, r), dev_x)
        wx[r].start()
        wy[r] = remote(spot(0, r), spot(0, r), dev_y)
        wy[r].start()
        to_sibling(0, r)

    loads[0].wait()
    send_own(0)

    def grad(i):
        part = lax.dot_general(tok[:, cols(order[i])], og[...], ROWS_ROWS, preferred_element_type=f32)
        part += lax.dot_general(tsib[i], osib[...], ROWS_ROWS, preferred_element_type=f32)
        return part * scale

    def relay(r):
        wx[r].wait_recv()
        to_sibling(1, r)
        wy[r].wait_recv()
        to_sibling(2, r)

    def diagonal():
        low, high = pl.ds(0, rows // 2), pl.ds(rows // 2, rows // 2)
        wx[0].wait_recv()
        part = wf.at[nx, z, low]
        d_low = remote(part, part, dev_y)
        d_low.start()
        wy[0].wait_recv()
        part = wf.at[ny, z, high]
        d_high = remote(part, part, dev_x)
        d_high.start()
        return d_low, d_high

    def diagonal_along_z():
        d_low.wait_recv()
        d_high.wait_recv()
        for k in (1, 3, 2):
            wd[k] = remote(spot(3, 0), spot(3, 0), dev_z[k])
            wd[k].start()
        to_sibling(1, 0)
        to_sibling(2, 0)
        to_sibling(3, 0)

    loads[1].wait()
    loads[2].wait()
    og_x.wait_recv()

    a1 = [[remote(sA.at[i, j], rA.at[i, j], dev_x) for j in (0, 1)] for i in (0, 1)]
    b1 = [[remote(sB.at[i, j], rB.at[i, j], dev_y) for j in (0, 1)] for i in (0, 1)]
    a2 = [remote(s2.at[0, j], r2.at[0, j], dev_y) for j in (0, 1)]
    b2 = [remote(s2.at[1, j], r2.at[1, j], dev_x) for j in (0, 1)]

    def left(j):
        return slice(j * quarter, (j + 1) * quarter)

    def right(j):
        return slice(half + j * quarter, half + (j + 1) * quarter)

    tok_x[0].wait_recv()
    g = grad(0)
    for j in (0, 1):
        sA[0, j] = g[:, left(j)].astype(bf16)
        sB[0, j] = g[:, right(j)].astype(bf16)
    a1[0][0].start()
    b1[0][0].start()
    d_low, d_high = diagonal()
    tok_x[1].wait_recv()
    g = grad(1)
    for j in (0, 1):
        sA[1, j] = g[:, left(j)].astype(bf16)
        g1b[j] = g[:, right(j)]
    a1[1][0].start()
    tok_x[2].wait_recv()
    g = grad(2)
    for j in (0, 1):
        sB[1, j] = g[:, right(j)].astype(bf16)
        g2a[j] = g[:, left(j)]
    b1[1][0].start()
    a1[0][1].start()
    b1[0][1].start()
    tok_x[3].wait_recv()
    g = grad(3)
    for j in (0, 1):
        g3[j, :, :quarter] = g[:, left(j)]
        g3[j, :, quarter:] = g[:, right(j)]

    def second(j):
        a1[0][j].wait_recv()
        s2[0, j] = (g2a[j] + rA[0, j].astype(f32)).astype(bf16)
        a2[j].start()
        b1[0][j].wait_recv()
        s2[1, j] = (g1b[j] + rB[0, j].astype(f32)).astype(bf16)
        b2[j].start()

    gz = {}

    def along_z(j):
        a1[1][j].wait_recv()
        b1[1][j].wait_recv()
        a2[j].wait_recv()
        b2[j].wait_recv()
        g3[j, :, :quarter] += rA[1, j].astype(f32) + r2[0, j].astype(f32)
        g3[j, :, quarter:] += rB[1, j].astype(f32) + r2[1, j].astype(f32)
        zs[j] = g3[j].astype(bf16).reshape(4, rows, half)
        for k in (1, 3, 2):
            gz[j, k] = remote(zs.at[j, (z + k) % 4], zr.at[j, k - 1], dev_z[k])
            gz[j, k].start()

    diagonal_along_z()
    second(0)
    a1[1][1].start()
    b1[1][1].start()
    second(1)
    wz[1].wait_recv()
    send_own(1)
    wz[3].wait_recv()
    send_own(3)
    wz[2].wait_recv()
    send_own(2)
    along_z(0)

    stores = []

    def use(n, first=False):
        w = wf[n].reshape(group, width)
        part = jnp.dot(tok[:, cols(n)], w, preferred_element_type=f32)
        if first:
            acc[...] = part
        else:
            acc[...] += part
        i = len(stores)
        ig[i] = lax.dot_general(og[...], w, COLS_COLS, preferred_element_type=f32).astype(bf16)
        store = pltpu.make_async_copy(ig.at[i], ig_h.at[:, cols(n)], osem.at[i])
        store.start()
        stores.append(store)

    def use_sibling(q):
        for r in range(4):
            wc[q, r].wait_recv()
        use(quad[q] + sib)

    along_z(1)

    relay(1)
    relay(3)
    relay(2)
    use(node, True)
    use_sibling(0)
    for r in (1, 3, 2):
        wd[r].wait_recv()
        to_sibling(3, r)
    use(nx)
    use(ny)
    use_sibling(1)
    use_sibling(2)

    own = pl.ds(pl.multiple_of(z * rows, 16), rows)
    for j in (0, 1):
        for k in (1, 3, 2):
            gz[j, k].wait_recv()
        total = g3[j, own, :] + zr[j, 0].astype(f32) + zr[j, 1].astype(f32) + zr[j, 2].astype(f32)
        wg_o[:, left(j)] = total[:, :quarter].astype(bf16)
        wg_o[:, right(j)] = total[:, quarter:].astype(bf16)

    use(nd)
    use_sibling(3)
    proj_o[...] = acc[...].astype(bf16)

    for copy in started:
        copy.wait_send()
    for store in stores:
        store.wait()


def hand_on(a, b, c, a_out, b_out, c_out, sem):
    pairs = ((a, a_out), (b, b_out), (c, c_out))
    copies = [pltpu.make_async_copy(src, dst, sem.at[i]) for i, (src, dst) in enumerate(pairs)]
    for copy in copies:
        copy.start()
    for copy in copies:
        copy.wait()


COPIES = 1 + 4 + 3 + 4 + 4 + 5 + 16 + 8 + 4 + 6


def fused(tokens, out_grad, weights):
    toks, features = tokens.shape
    rows, width = weights.shape
    devices = lax.axis_size("node") * lax.axis_size("local")
    scale = 1.0 / float(toks * devices) ** 0.5
    group, half, quarter = 4 * rows, width // 2, width // 4
    bf16, f32 = jnp.bfloat16, jnp.float32
    results = pl.pallas_call(
        functools.partial(kernel, scale),
        out_shape=(
            jax.ShapeDtypeStruct((toks, width), bf16),
            jax.ShapeDtypeStruct((toks, features), bf16),
            jax.ShapeDtypeStruct((rows, width), bf16),
        ),
        in_specs=[pl.BlockSpec(memory_space=pltpu.HBM)] * 3,
        out_specs=(
            pl.BlockSpec(memory_space=pltpu.VMEM),
            pl.BlockSpec(memory_space=pl.ANY),
            pl.BlockSpec(memory_space=pltpu.VMEM),
        ),
        scratch_shapes=[
            pltpu.VMEM((toks, features), bf16),
            pltpu.VMEM((toks, width), bf16),
            pltpu.VMEM((4, toks, group), bf16),
            pltpu.VMEM((toks, width), bf16),
            pltpu.VMEM((8, 4, rows, width), bf16),
            pltpu.VMEM((toks, width), f32),
            pltpu.VMEM((8, toks, group), bf16),
            pltpu.VMEM((2, group, quarter), f32),
            pltpu.VMEM((2, group, quarter), f32),
            pltpu.VMEM((2, group, half), f32),
            pltpu.VMEM((2, 2, group, quarter), bf16),
            pltpu.VMEM((2, 2, group, quarter), bf16),
            pltpu.VMEM((2, 2, group, quarter), bf16),
            pltpu.VMEM((2, 2, group, quarter), bf16),
            pltpu.VMEM((2, 2, group, quarter), bf16),
            pltpu.VMEM((2, 2, group, quarter), bf16),
            pltpu.VMEM((2, 4, rows, half), bf16),
            pltpu.VMEM((2, 3, rows, half), bf16),
            pltpu.SemaphoreType.DMA((3,)),
            pltpu.SemaphoreType.DMA((COPIES,)),
            pltpu.SemaphoreType.DMA((COPIES,)),
            pltpu.SemaphoreType.DMA((8,)),
        ],
        compiler_params=pltpu.CompilerParams(
            collective_id=0, has_side_effects=True, vmem_limit_bytes=40 * 2**20),
        cost_estimate=pl.CostEstimate(
            flops=6 * toks * features * width, bytes_accessed=2 * toks * features * 4, transcendentals=0),
    )(tokens, out_grad, weights)
    return pl.pallas_call(
        hand_on,
        out_shape=tuple(jax.ShapeDtypeStruct(a.shape, a.dtype) for a in results),
        in_specs=[pl.BlockSpec(memory_space=pl.ANY)] * 3,
        out_specs=[pl.BlockSpec(memory_space=pl.ANY)] * 3,
        scratch_shapes=[pltpu.SemaphoreType.DMA((3,))],
        compiler_params=pltpu.CompilerParams(vmem_limit_bytes=2**20),
    )(*results)


def plain(tokens, out_grad, weights):
    tok_rows = tokens.shape[0]
    devices = lax.axis_size("node") * lax.axis_size("local")
    grad_scale = 1.0 / jnp.sqrt(jnp.float32(tok_rows * devices))
    grad_term = lax.dot_general(tokens, out_grad, ROWS_ROWS, preferred_element_type=jnp.float32)
    grad_term = (grad_term * grad_scale).astype(jnp.bfloat16)
    grad_term = lax.optimization_barrier(grad_term).astype(jnp.float32)
    shard_rows = lax.all_gather(weights, ("node", "local"), axis=0, tiled=True)
    projected = jnp.dot(tokens, shard_rows, preferred_element_type=jnp.float32).astype(jnp.bfloat16)
    input_grad = lax.dot_general(
        out_grad, shard_rows, COLS_COLS, preferred_element_type=jnp.float32).astype(jnp.bfloat16)
    across = lax.psum_scatter(grad_term, "node", scatter_dimension=0, tiled=True)
    summed = lax.psum_scatter(across, "local", scatter_dimension=0, tiled=True)
    return projected, input_grad, summed.astype(jnp.bfloat16)


def solution(mesh):
    spec = P(("node", "local"), None)
    fits = mesh.shape["node"] == 8 and mesh.shape["local"] == 4
    return jax.shard_map(
        fused if fits else plain,
        mesh=mesh,
        in_specs=(spec, spec, spec),
        out_specs=(spec, spec, spec),
        check_vma=False,
    )
```
